32 devices in a mesh: tok: 8 (over y, x, core), ch: 4 (over z).
Axes of the slice: x: 2, y: 2, z: 4, core: 2. Of those that a mesh axis runs over, the one named last changes fastest.
Arguments:
- activations: bfloat16 [2048, 8192], P('tok', 'ch'), may hold values from -25 to 25
- weight: bfloat16 [14336, 8192], P('tok', 'ch'), may hold values from -0.0625 to 0.0625
- basis: bfloat16 [1024, 8192], P(None, 'ch'), may hold values from -0.0625 to 0.0625
Outputs:
- left_factor: float32 [14336, 1024], P(('tok', 'ch'))
The draws below stay inside these ranges and needn't reach their ends.
All inputs are finite; a program needn't handle non-finite values.
Results may differ from the reference program's by a relative error of at most 0.0088.
Values sent between devices are 32-bit elements; how exact they have to be, the bound alone decides.
A program may use at most 128 MiB of HBM per device.

```python
import jax
import jax.numpy as jnp
from jax import lax

IN_CH = 8192
OUT_ROWS = 14336
RANK = 1024
TOKENS = 2048


def draw_activations(key, part):
    key = jax.random.fold_in(key, 11)
    subkeys = jax.random.split(key, 4)
    position = jnp.arange(TOKENS, dtype=jnp.float32) / TOKENS
    row_scale = 10.0 ** jax.random.uniform(subkeys[0], (TOKENS, 1)) * jnp.sqrt((1.0 + 2.0 * position[:, None]) / 3.0)
    col_scale = 10.0 ** (jax.random.uniform(subkeys[1], (1, IN_CH)) * 0.5 - 0.25)
    entries = jax.random.truncated_normal(subkeys[3], -4.0, 4.0, (TOKENS, IN_CH))
    return (entries * row_scale * col_scale / 3.0).astype(jnp.bfloat16)


def steps_of(key, shape, cuts, low, top_value):
    level, own = 1.0, jax.random.fold_in(key, 6)
    for dim, parts in cuts:
        heights = jnp.exp(jax.random.uniform(jax.random.fold_in(own, dim), (parts,), jnp.float32, low / len(cuts), top_value / len(cuts)))
        level = level * jnp.repeat(heights, shape[dim] // parts).reshape([-1 if axis == dim else 1 for axis in range(len(shape))])
    return level


def bell_draw(key, dims, spread, bound, cuts=(), kind=jnp.bfloat16):
    drawn = jax.random.normal(key, dims, jnp.float32) * spread
    if len(cuts) > 0:
        drawn = steps_of(key, dims, cuts, -0.22, 0.18) * drawn
    return jnp.clip(drawn, min=-bound, max=bound).astype(kind)


def setup_inputs(seed: int = 0) -> dict:
    key_list = jax.random.split(jax.random.key(seed), 4)
    return {
        "activations": draw_activations(jax.random.fold_in(key_list[3], 71), 0),
        "weight": bell_draw(key_list[1], (OUT_ROWS, IN_CH), IN_CH ** -0.5, 0.0625, ((0, 8), (1, 4))),
        "basis": bell_draw(key_list[2], (RANK, IN_CH), IN_CH ** -0.5, 0.0625, ((1, 4),)),
    }


damping = 0.1

def reference(activations, weight, basis):
    codes = lax.dot_general(activations.astype(jnp.float32), basis.astype(jnp.float32), (((1,), (1,)), ((), ())), preferred_element_type=jnp.float32)
    gram = lax.dot_general(codes.astype(jnp.float32), codes.astype(jnp.float32), (((0,), (0,)), ((), ())), precision=lax.Precision.HIGHEST, preferred_element_type=jnp.float32)
    codes_low = codes.astype(jnp.bfloat16)
    moments = lax.dot_general(activations.astype(jnp.float32), codes_low.astype(jnp.float32), (((0,), (0,)), ((), ())), preferred_element_type=jnp.float32)
    cross = jnp.dot(weight.astype(jnp.float32), moments.astype(jnp.float32), precision=lax.Precision.HIGHEST, preferred_element_type=jnp.float32)
    ridge = damping * jnp.trace(gram) / RANK
    damped = gram + ridge * jnp.eye(RANK, dtype=jnp.float32)
    lower = jnp.linalg.cholesky(damped)
    middle = jax.scipy.linalg.solve_triangular(lower, cross.T, lower=True)
    solved = jax.scipy.linalg.solve_triangular(lower, middle, trans=1, lower=True)
    return solved.T
```

```python
import jax
import jax.numpy as jnp
from jax import lax
from jax.experimental import pallas as pl
from jax.experimental.pallas import tpu as pltpu
from jax.sharding import PartitionSpec as P

damping = 0.1
block = 128
group = 4
HIGHEST = lax.Precision.HIGHEST


def dot_f32(a, b, dims=(((1,), (0,)), ((), ()))):
    return lax.dot_general(a, b, dims, precision=HIGHEST, preferred_element_type=jnp.float32)


NT = (((1,), (1,)), ((), ()))


def factor_inverse(a):
    n = a.shape[0]
    tiles = n // 8
    lanes = lax.broadcasted_iota(jnp.int32, (8, n), 1)
    subs = lax.broadcasted_iota(jnp.int32, (8, n), 0)
    left = [a[8 * t : 8 * t + 8] for t in range(tiles)]
    right = [(lanes == subs + 8 * t).astype(jnp.float32) for t in range(tiles)]
    for start in range(0, n, group):
        first = start // 8
        base = start - 8 * first
        rows = [
            (left[first][base + g : base + g + 1], right[first][base + g : base + g + 1])
            for g in range(group)
        ]
        cols = {
            t: [
                jnp.broadcast_to(left[t][:, start + g : start + g + 1], (8, n))
                for g in range(group)
            ]
            for t in range(first, tiles)
        }
        small = [
            [cols[first][h][base + g : base + g + 1] for h in range(group)] for g in range(group)
        ]
        inverse = []
        factors = [[None] * group for _ in range(group)]
        for g in range(group):
            inverse.append(1.0 / small[g][g])
            for h in range(g + 1, group):
                f = small[h][g] * inverse[g]
                factors[h][g] = f
                for k in range(g + 1, group):
                    small[h][k] = small[h][k] - f * small[g][k]
                rows[h] = (rows[h][0] - f * rows[g][0], rows[h][1] - f * rows[g][1])
        scaled = [small[g] for g in range(group)]
        for t in range(first, tiles):
            mults = []
            for g in range(group):
                c = cols[t][g]
                for k in range(g):
                    c = c - mults[k] * scaled[k][g]
                m = c * inverse[g]
                if t == first:
                    m = jnp.where(subs > base + g, m, 0.0)
                mults.append(m)
            for g in range(group):
                left[t] = left[t] - mults[g] * rows[g][0]
                right[t] = right[t] - mults[g] * rows[g][1]
    out = []
    for t in range(tiles):
        pivot = jnp.sum(
            jnp.where(lanes == subs + 8 * t, left[t], 0.0), axis=1, keepdims=True
        )
        out.append(right[t] * (1.0 / jnp.sqrt(pivot)))
    return jnp.concatenate(out, axis=0)


def inverse_factor_kernel(gram_ref, out_ref, work, diag):
    n = gram_ref.shape[0]
    steps = n // block
    trace = jnp.zeros((1, 1), jnp.float32)
    eye = lax.broadcasted_iota(jnp.int32, (block, block), 0) == lax.broadcasted_iota(
        jnp.int32, (block, block), 1
    )
    for k in range(steps):
        s = slice(k * block, (k + 1) * block)
        trace += jnp.sum(jnp.where(eye, gram_ref[s, s], 0.0), keepdims=True)
    ridge = damping * trace / n
    work[...] = gram_ref[...]
    for k in range(steps):
        s = slice(k * block, (k + 1) * block)
        work[s, s] = gram_ref[s, s] + jnp.where(eye, ridge, 0.0)

    def step(k, carry):
        o = pl.multiple_of(k * block, block)
        diag[...] = factor_inverse(work[pl.ds(o, block), pl.ds(o, block)])
        for kk in range(steps):

            @pl.when(k == kk)
            def _(kk=kk):
                s = slice(kk * block, (kk + 1) * block)
                inv = diag[...]
                row = dot_f32(inv, work[s, :])
                work[s, :] = row
                work[s, s] = inv
                row = work[s, :]
                for t in range(kk + 1, steps):
                    r = slice(t * block, (t + 1) * block)
                    mult = dot_f32(work[r, s], inv, NT)
                    work[r, s] = jnp.zeros((block, block), jnp.float32)
                    work[r, :] = work[r, :] - dot_f32(mult, row)

        return carry

    lax.fori_loop(0, steps, step, 0)
    for k in range(steps):
        s = slice(k * block, (k + 1) * block)
        if k:
            out_ref[s, : k * block] = work[s, : k * block]
        out_ref[s, s] = work[s, s]
        if k + 1 < steps:
            out_ref[s, (k + 1) * block :] = jnp.zeros((block, n - (k + 1) * block), jnp.float32)


def inverse_factor(gram):
    n = gram.shape[0]
    return pl.pallas_call(
        inverse_factor_kernel,
        out_shape=jax.ShapeDtypeStruct((n, n), jnp.float32),
        in_specs=[pl.BlockSpec(memory_space=pltpu.VMEM)],
        out_specs=pl.BlockSpec(memory_space=pltpu.VMEM),
        scratch_shapes=[
            pltpu.VMEM((n, n), jnp.float32),
            pltpu.VMEM((block, block), jnp.float32),
        ],
        compiler_params=pltpu.CompilerParams(vmem_limit_bytes=32 * 1024 * 1024),
        cost_estimate=pl.CostEstimate(
            flops=100_000_000_000, bytes_accessed=8 * n * n, transcendentals=0
        ),
        name="inverse_factor",
    )(gram)


def shards(activations, weight, basis):
    partial_value = lax.dot_general(
        activations, basis, (((1,), (1,)), ((), ())), preferred_element_type=jnp.float32
    )
    codes = lax.psum(partial_value, "ch")
    local_gram = dot_f32(codes, codes, (((0,), (0,)), ((), ())))
    gram = lax.psum(local_gram, "tok")
    codes_low = codes.astype(jnp.bfloat16)
    local_moments = lax.dot_general(
        activations, codes_low, (((0,), (0,)), ((), ())), preferred_element_type=jnp.float32
    )
    gram, local_moments = lax.optimization_barrier((gram, local_moments))
    inverse = inverse_factor(gram)
    moments = lax.psum(local_moments, "tok")
    high = lax.reduce_precision(moments, 8, 7)
    rest = (moments - high).astype(jnp.bfloat16)
    high = high.astype(jnp.bfloat16)
    cross = lax.psum_scatter(
        jnp.dot(weight, high, preferred_element_type=jnp.float32)
        + jnp.dot(weight, rest, preferred_element_type=jnp.float32),
        "ch",
        scatter_dimension=0,
        tiled=True,
    )
    middle = lax.dot_general(
        cross, inverse, NT, precision=lax.Precision.HIGH, preferred_element_type=jnp.float32
    )
    return jnp.dot(
        middle, inverse, precision=lax.Precision.HIGH, preferred_element_type=jnp.float32
    )


def solution(mesh):
    in_specs = (P("tok", "ch"), P("tok", "ch"), P(None, "ch"))
    out_specs = P(("tok", "ch"), None)
    return jax.shard_map(shards, mesh=mesh, in_specs=in_specs, out_specs=out_specs, check_vma=False)
```

```python
import functools
import math

import jax
import jax.numpy as jnp
from jax import lax
from jax.experimental import pallas as pl
from jax.experimental.pallas import tpu as pltpu
from jax.sharding import PartitionSpec as P

damping = 0.1
block = 128
group = 4
HIGHEST = lax.Precision.HIGHEST


def dot_f32(a, b, dims=(((1,), (0,)), ((), ()))):
    return lax.dot_general(a, b, dims, precision=HIGHEST, preferred_element_type=jnp.float32)


NT = (((1,), (1,)), ((), ()))


def factor_inverse(a):
    n = a.shape[0]
    tiles = n // 8
    lanes = lax.broadcasted_iota(jnp.int32, (8, n), 1)
    subs = lax.broadcasted_iota(jnp.int32, (8, n), 0)
    left = [a[8 * t : 8 * t + 8] for t in range(tiles)]
    right = [(lanes == subs + 8 * t).astype(jnp.float32) for t in range(tiles)]
    for start in range(0, n, group):
        first = start // 8
        base = start - 8 * first
        rows = [
            (left[first][base + g : base + g + 1], right[first][base + g : base + g + 1])
            for g in range(group)
        ]
        cols = {
            t: [
                jnp.broadcast_to(left[t][:, start + g : start + g + 1], (8, n))
                for g in range(group)
            ]
            for t in range(first, tiles)
        }
        small = [
            [cols[first][h][base + g : base + g + 1] for h in range(group)] for g in range(group)
        ]
        inverse = []
        factors = [[None] * group for _ in range(group)]
        for g in range(group):
            inverse.append(1.0 / small[g][g])
            for h in range(g + 1, group):
                f = small[h][g] * inverse[g]
                factors[h][g] = f
                for k in range(g + 1, group):
                    small[h][k] = small[h][k] - f * small[g][k]
                rows[h] = (rows[h][0] - f * rows[g][0], rows[h][1] - f * rows[g][1])
        scaled = [small[g] for g in range(group)]
        for t in range(first, tiles):
            mults = []
            for g in range(group):
                c = cols[t][g]
                for k in range(g):
                    c = c - mults[k] * scaled[k][g]
                m = c * inverse[g]
                if t == first:
                    m = jnp.where(subs > base + g, m, 0.0)
                mults.append(m)
            for g in range(group):
                left[t] = left[t] - mults[g] * rows[g][0]
                right[t] = right[t] - mults[g] * rows[g][1]
    out = []
    for t in range(tiles):
        pivot = jnp.sum(
            jnp.where(lanes == subs + 8 * t, left[t], 0.0), axis=1, keepdims=True
        )
        out.append(right[t] * (1.0 / jnp.sqrt(pivot)))
    return jnp.concatenate(out, axis=0)


def inverse_factor_kernel(gram_ref, out_ref, work, diag):
    n = gram_ref.shape[0]
    steps = n // block
    trace = jnp.zeros((1, 1), jnp.float32)
    eye = lax.broadcasted_iota(jnp.int32, (block, block), 0) == lax.broadcasted_iota(
        jnp.int32, (block, block), 1
    )
    for k in range(steps):
        s = slice(k * block, (k + 1) * block)
        trace += jnp.sum(jnp.where(eye, gram_ref[s, s], 0.0), keepdims=True)
    ridge = damping * trace / n
    work[...] = gram_ref[...]
    for k in range(steps):
        s = slice(k * block, (k + 1) * block)
        work[s, s] = gram_ref[s, s] + jnp.where(eye, ridge, 0.0)

    def step(k, carry):
        o = pl.multiple_of(k * block, block)
        diag[...] = factor_inverse(work[pl.ds(o, block), pl.ds(o, block)])
        for kk in range(steps):

            @pl.when(k == kk)
            def _(kk=kk):
                s = slice(kk * block, (kk + 1) * block)
                inv = diag[...]
                row = dot_f32(inv, work[s, :])
                work[s, :] = row
                work[s, s] = inv
                row = work[s, :]
                for t in range(kk + 1, steps):
                    r = slice(t * block, (t + 1) * block)
                    mult = dot_f32(work[r, s], inv, NT)
                    work[r, s] = jnp.zeros((block, block), jnp.float32)
                    work[r, :] = work[r, :] - dot_f32(mult, row)

        return carry

    lax.fori_loop(0, steps, step, 0)
    for k in range(steps):
        s = slice(k * block, (k + 1) * block)
        if k:
            out_ref[s, : k * block] = work[s, : k * block]
        out_ref[s, s] = work[s, s]
        if k + 1 < steps:
            out_ref[s, (k + 1) * block :] = jnp.zeros((block, n - (k + 1) * block), jnp.float32)


def inverse_factor(gram):
    n = gram.shape[0]
    return pl.pallas_call(
        inverse_factor_kernel,
        out_shape=jax.ShapeDtypeStruct((n, n), jnp.float32),
        in_specs=[pl.BlockSpec(memory_space=pltpu.VMEM)],
        out_specs=pl.BlockSpec(memory_space=pltpu.VMEM),
        scratch_shapes=[
            pltpu.VMEM((n, n), jnp.float32),
            pltpu.VMEM((block, block), jnp.float32),
        ],
        compiler_params=pltpu.CompilerParams(vmem_limit_bytes=32 * 1024 * 1024),
        cost_estimate=pl.CostEstimate(
            flops=10_000_000_000, bytes_accessed=8 * n * n, transcendentals=0
        ),
        name="inverse_factor",
    )(gram)


def all_reduce_kernel(axis, size, parts, x_ref, out_ref, acc, *rest):
    bits = size.bit_length() - 1
    land, (send, recv) = rest[:bits], rest[bits:]
    rows = x_ref.shape[0] // parts
    me = lax.axis_index(axis)
    bit = [lax.rem(me // (1 << b), 2) for b in range(bits)]
    peer = [me + (1 - 2 * bit[b]) * (1 << b) for b in range(bits)]

    barrier = pltpu.get_barrier_semaphore()
    for b in range(bits):
        pl.semaphore_signal(
            barrier, inc=1, device_id={axis: peer[b]}, device_id_type=pl.DeviceIdType.MESH
        )
    pl.semaphore_wait(barrier, bits)

    orders = []
    for p in range(parts):
        order = list(range(bits))
        if p % 2:
            order[-2:] = order[-2:][::-1]
        orders.append(order)
    starts = [[p * rows + jnp.int32(0)] for p in range(parts)]
    for p in range(parts):
        for s in range(bits):
            starts[p].append(starts[p][-1] + bit[orders[p][s]] * (rows >> (s + 1)))

    def copy(src, dst, p, s, phase):
        return pltpu.make_async_remote_copy(
            src_ref=src,
            dst_ref=dst,
            send_sem=send.at[phase, p, s],
            recv_sem=recv.at[phase, p, s],
            device_id={axis: peer[orders[p][s]]},
            device_id_type=pl.DeviceIdType.MESH,
        )

    def region(start, length):
        return pl.ds(pl.multiple_of(start, 8), length)

    def halve(p, s):
        length = rows >> (s + 1)
        away = starts[p][s] + (1 - bit[orders[p][s]]) * length
        src = x_ref if s == 0 else acc
        c = copy(src.at[region(away, length)], land[s].at[pl.ds(p * length, length)], p, s, 0)
        c.start()
        return c

    def add(p, s):
        length = rows >> (s + 1)
        src = x_ref if s == 0 else acc
        dst = out_ref if s == bits - 1 else acc
        chunk = min(length, 32)

        def body(i, carry):
            own = region(starts[p][s + 1] + i * chunk, chunk)
            dst[own] = src[own] + land[s][region(p * length + i * chunk, chunk)]
            return carry

        lax.fori_loop(0, length // chunk, body, 0)

    def double(p, s):
        own = region(starts[p][s + 1], rows >> (s + 1))
        c = copy(out_ref.at[own], out_ref.at[own], p, s, 1)
        c.start()
        return c

    started = []
    flying = [halve(p, 0) for p in range(parts)]
    for s in range(bits):
        for p in range(parts):
            flying[p].wait_recv()
            add(p, s)
            started.append(flying[p])
            flying[p] = halve(p, s + 1) if s + 1 < bits else double(p, s)
    for s in range(bits - 1, -1, -1):
        for p in range(parts):
            flying[p].wait_recv()
            started.append(flying[p])
            if s:
                flying[p] = double(p, s - 1)
    for c in started:
        c.wait_send()


def all_reduce(x, axis, size, parts, collective_id):
    bits = size.bit_length() - 1
    rows, cols = x.shape
    scratch = [pltpu.VMEM((rows, cols), jnp.float32)]
    scratch += [pltpu.VMEM((rows >> (s + 1), cols), jnp.float32) for s in range(bits)]
    scratch += [pltpu.SemaphoreType.DMA((2, parts, bits))] * 2
    return pl.pallas_call(
        functools.partial(all_reduce_kernel, axis, size, parts),
        out_shape=jax.ShapeDtypeStruct((rows, cols), jnp.float32),
        in_specs=[pl.BlockSpec(memory_space=pltpu.VMEM)],
        out_specs=pl.BlockSpec(memory_space=pltpu.VMEM),
        scratch_shapes=scratch,
        compiler_params=pltpu.CompilerParams(
            collective_id=collective_id,
            has_side_effects=True,
            vmem_limit_bytes=16 * rows * cols + 4 * 1024 * 1024,
        ),
        cost_estimate=pl.CostEstimate(
            flops=rows * cols * 20_000, bytes_accessed=8 * rows * cols, transcendentals=0
        ),
        name="all_reduce_" + str(collective_id),
    )(x)


def cross_kernel(weight_ref, moments_ref, out_ref, high, rest):
    depth = moments_ref.shape[0]
    chunk = 128

    @pl.when(pl.program_id(0) == 0)
    def _():
        def body(i, carry):
            s = pl.ds(pl.multiple_of(i * chunk, chunk), chunk)
            value = moments_ref[s]
            top = value.astype(jnp.bfloat16)
            high[s] = top
            rest[s] = (value - top.astype(jnp.float32)).astype(jnp.bfloat16)
            return carry

        lax.fori_loop(0, depth // chunk, body, 0)

    rows = weight_ref[...]
    out_ref[...] = jnp.dot(rows, high[...], preferred_element_type=jnp.float32) + jnp.dot(
        rows, rest[...], preferred_element_type=jnp.float32
    )


def cross_product(weight, moments):
    rows, depth = weight.shape
    cols = moments.shape[1]
    tile = math.gcd(rows, 256)
    return pl.pallas_call(
        cross_kernel,
        grid=(rows // tile,),
        out_shape=jax.ShapeDtypeStruct((rows, cols), jnp.float32),
        in_specs=[
            pl.BlockSpec((tile, depth), lambda i: (i, 0)),
            pl.BlockSpec((depth, cols), lambda i: (0, 0)),
        ],
        out_specs=pl.BlockSpec((tile, cols), lambda i: (i, 0)),
        scratch_shapes=[pltpu.VMEM((depth, cols), jnp.bfloat16)] * 2,
        compiler_params=pltpu.CompilerParams(vmem_limit_bytes=24 * 1024 * 1024),
        cost_estimate=pl.CostEstimate(
            flops=4 * rows * depth * cols,
            bytes_accessed=2 * rows * depth + 4 * cols * (rows + depth),
            transcendentals=0,
        ),
        name="cross_product",
    )(weight, moments)


def shards(mesh, activations, weight, basis):
    tok, ch = mesh.shape["tok"], mesh.shape["ch"]
    partial_value = lax.dot_general(
        activations, basis, (((1,), (1,)), ((), ())), preferred_element_type=jnp.float32
    )
    codes = all_reduce(partial_value, "ch", ch, 2, 1)
    codes_low = codes.astype(jnp.bfloat16)
    half = codes.shape[1] // 2

    def moments_of(c):
        return lax.dot_general(
            activations,
            codes_low[:, c * half : (c + 1) * half],
            (((0,), (0,)), ((), ())),
            preferred_element_type=jnp.float32,
        )

    def cross_of(moments):
        return cross_product(weight, moments)

    def scatter(part):
        return lax.psum_scatter(part, "ch", scatter_dimension=0, tiled=True)

    first = cross_of(all_reduce(moments_of(0), "tok", tok, 4, 2))
    first, local = lax.optimization_barrier((first, moments_of(1)))
    cross_first = scatter(first)
    second = cross_of(all_reduce(local, "tok", tok, 4, 2))
    local_gram = dot_f32(codes, codes, (((0,), (0,)), ((), ())))
    second, local_gram, cross_first = lax.optimization_barrier((second, local_gram, cross_first))
    cross_second = scatter(second)
    inverse = inverse_factor(all_reduce(local_gram, "tok", tok, 4, 3))

    def high_dot(a, b, dims):
        return lax.dot_general(
            a, b, dims, precision=lax.Precision.HIGH, preferred_element_type=jnp.float32
        )

    middle = high_dot(cross_first, inverse[:, :half], NT) + high_dot(
        cross_second, inverse[:, half:], NT
    )
    return high_dot(middle, inverse, (((1,), (0,)), ((), ())))


def solution(mesh):
    in_specs = (P("tok", "ch"), P("tok", "ch"), P(None, "ch"))
    out_specs = P(("tok", "ch"), None)
    return jax.shard_map(
        functools.partial(shards, mesh),
        mesh=mesh,
        in_specs=in_specs,
        out_specs=out_specs,
        check_vma=False,
    )
```

```python
import functools
import math

import jax
import jax.numpy as jnp
from jax import lax
from jax.experimental import pallas as pl
from jax.experimental.pallas import tpu as pltpu
from jax.sharding import PartitionSpec as P

damping = 0.1
block = 128
group = 8
pack = 256
HIGHEST = lax.Precision.HIGHEST


def dot_f32(a, b, dims=(((1,), (0,)), ((), ()))):
    return lax.dot_general(a, b, dims, precision=HIGHEST, preferred_element_type=jnp.float32)


NT = (((1,), (1,)), ((), ()))


def factor_inverse(a):
    n = a.shape[0]
    tiles = n // 8
    lanes = lax.broadcasted_iota(jnp.int32, (8, n), 1)
    subs = lax.broadcasted_iota(jnp.int32, (8, n), 0)
    left = [a[8 * t : 8 * t + 8] for t in range(tiles)]
    right = [(lanes == subs + 8 * t).astype(jnp.float32) for t in range(tiles)]
    for start in range(0, n, group):
        first = start // 8
        base = start - 8 * first
        rows = [
            (left[first][base + g : base + g + 1], right[first][base + g : base + g + 1])
            for g in range(group)
        ]
        cols = {
            t: [
                jnp.broadcast_to(left[t][:, start + g : start + g + 1], (8, n))
                for g in range(group)
            ]
            for t in range(first, tiles)
        }
        small = [
            [cols[first][h][base + g : base + g + 1] for h in range(group)] for g in range(group)
        ]
        inverse = []
        factors = [[None] * group for _ in range(group)]
        for g in range(group):
            inverse.append(1.0 / small[g][g])
            for h in range(g + 1, group):
                f = small[h][g] * inverse[g]
                factors[h][g] = f
                for k in range(g + 1, group):
                    small[h][k] = small[h][k] - f * small[g][k]
                rows[h] = (rows[h][0] - f * rows[g][0], rows[h][1] - f * rows[g][1])
        scaled = [small[g] for g in range(group)]
        for t in range(first, tiles):
            mults = []
            for g in range(group):
                c = cols[t][g]
                for k in range(g):
                    c = c - mults[k] * scaled[k][g]
                m = c * inverse[g]
                if t == first:
                    m = jnp.where(subs > base + g, m, 0.0)
                mults.append(m)
            for g in range(group):
                left[t] = left[t] - mults[g] * rows[g][0]
                right[t] = right[t] - mults[g] * rows[g][1]
    out = []
    for t in range(tiles):
        pivot = jnp.sum(
            jnp.where(lanes == subs + 8 * t, left[t], 0.0), axis=1, keepdims=True
        )
        out.append(right[t] * (1.0 / jnp.sqrt(pivot)))
    return jnp.concatenate(out, axis=0)


def inverse_factor_kernel(packed_ref, out_ref, work, diag):
    n = work.shape[0]
    steps = n // block
    offset = 0
    for j in range(0, n, pack):
        work[j:, j : j + pack] = packed_ref[offset : offset + n - j]
        for i in range(j + pack, n, pack):
            at = offset + i - j
            work[j : j + pack, i : i + pack] = packed_ref[at : at + pack].T
        offset += n - j
    trace = jnp.zeros((1, 1), jnp.float32)
    eye = lax.broadcasted_iota(jnp.int32, (block, block), 0) == lax.broadcasted_iota(
        jnp.int32, (block, block), 1
    )
    for k in range(steps):
        s = slice(k * block, (k + 1) * block)
        trace += jnp.sum(jnp.where(eye, work[s, s], 0.0), keepdims=True)
    ridge = damping * trace / n
    for k in range(steps):
        s = slice(k * block, (k + 1) * block)
        work[s, s] = work[s, s] + jnp.where(eye, ridge, 0.0)

    def step(k, carry):
        o = pl.multiple_of(k * block, block)
        diag[...] = factor_inverse(work[pl.ds(o, block), pl.ds(o, block)])
        for kk in range(steps):

            @pl.when(k == kk)
            def _(kk=kk):
                s = slice(kk * block, (kk + 1) * block)
                inv = diag[...]
                row = dot_f32(inv, work[s, :])
                work[s, :] = row
                work[s, s] = inv
                row = work[s, :]
                if kk + 1 < steps:
                    below = slice((kk + 1) * block, n)
                    mult = dot_f32(work[below, s], inv, NT)
                    work[below, s] = jnp.zeros((n - (kk + 1) * block, block), jnp.float32)
                    work[below, :] = work[below, :] - dot_f32(mult, row)

        return carry

    lax.fori_loop(0, steps, step, 0)
    for k in range(steps):
        s = slice(k * block, (k + 1) * block)
        if k:
            out_ref[s, : k * block] = work[s, : k * block]
        out_ref[s, s] = work[s, s]
        if k + 1 < steps:
            out_ref[s, (k + 1) * block :] = jnp.zeros((block, n - (k + 1) * block), jnp.float32)


def inverse_factor(packed, n):
    return pl.pallas_call(
        inverse_factor_kernel,
        out_shape=jax.ShapeDtypeStruct((n, n), jnp.float32),
        in_specs=[pl.BlockSpec(memory_space=pltpu.VMEM)],
        out_specs=pl.BlockSpec(memory_space=pltpu.VMEM),
        scratch_shapes=[
            pltpu.VMEM((n, n), jnp.float32),
            pltpu.VMEM((block, block), jnp.float32),
        ],
        compiler_params=pltpu.CompilerParams(vmem_limit_bytes=32 * 1024 * 1024),
        cost_estimate=pl.CostEstimate(
            flops=1_000_000_000, bytes_accessed=8 * n * n, transcendentals=0
        ),
        name="inverse_factor",
    )(packed)


def all_reduce_kernel(axis, size, parts, x_ref, out_ref, acc, *rest):
    bits = size.bit_length() - 1
    land, (send, recv) = rest[:bits], rest[bits:]
    rows = x_ref.shape[0] // parts
    me = lax.axis_index(axis)
    bit = [lax.rem(me // (1 << b), 2) for b in range(bits)]
    peer = [me + (1 - 2 * bit[b]) * (1 << b) for b in range(bits)]

    barrier = pltpu.get_barrier_semaphore()
    for b in range(bits):
        pl.semaphore_signal(
            barrier, inc=1, device_id={axis: peer[b]}, device_id_type=pl.DeviceIdType.MESH
        )
    pl.semaphore_wait(barrier, bits)

    orders = []
    for p in range(parts):
        order = list(range(bits))
        if p % 2:
            order[-2:] = order[-2:][::-1]
        orders.append(order)
    starts = [[p * rows + jnp.int32(0)] for p in range(parts)]
    for p in range(parts):
        for s in range(bits):
            starts[p].append(starts[p][-1] + bit[orders[p][s]] * (rows >> (s + 1)))

    def copy(src, dst, p, s, phase):
        return pltpu.make_async_remote_copy(
            src_ref=src,
            dst_ref=dst,
            send_sem=send.at[phase, p, s],
            recv_sem=recv.at[phase, p, s],
            device_id={axis: peer[orders[p][s]]},
            device_id_type=pl.DeviceIdType.MESH,
        )

    def region(start, length):
        return pl.ds(pl.multiple_of(start, 8), length)

    def halve(p, s):
        length = rows >> (s + 1)
        away = starts[p][s] + (1 - bit[orders[p][s]]) * length
        src = x_ref if s == 0 else acc
        c = copy(src.at[region(away, length)], land[s].at[pl.ds(p * length, length)], p, s, 0)
        c.start()
        return c

    def add(p, s):
        length = rows >> (s + 1)
        src = x_ref if s == 0 else acc
        dst = out_ref if s == bits - 1 else acc
        chunk = math.gcd(length, 32)

        def body(i, carry):
            own = region(starts[p][s + 1] + i * chunk, chunk)
            dst[own] = src[own] + land[s][region(p * length + i * chunk, chunk)]
            return carry

        lax.fori_loop(0, length // chunk, body, 0)

    def double(p, s):
        own = region(starts[p][s + 1], rows >> (s + 1))
        c = copy(out_ref.at[own], out_ref.at[own], p, s, 1)
        c.start()
        return c

    started = []
    flying = [halve(p, 0) for p in range(parts)]
    for s in range(bits):
        for p in range(parts):
            flying[p].wait_recv()
            add(p, s)
            started.append(flying[p])
            flying[p] = halve(p, s + 1) if s + 1 < bits else double(p, s)
    for s in range(bits - 1, -1, -1):
        for p in range(parts):
            flying[p].wait_recv()
            started.append(flying[p])
            if s:
                flying[p] = double(p, s - 1)
    for c in started:
        c.wait_send()


def all_reduce(x, axis, size, parts, collective_id):
    bits = size.bit_length() - 1
    rows, cols = x.shape
    scratch = [pltpu.VMEM((rows, cols), jnp.float32)]
    scratch += [pltpu.VMEM((rows >> (s + 1), cols), jnp.float32) for s in range(bits)]
    scratch += [pltpu.SemaphoreType.DMA((2, parts, bits))] * 2
    return pl.pallas_call(
        functools.partial(all_reduce_kernel, axis, size, parts),
        out_shape=jax.ShapeDtypeStruct((rows, cols), jnp.float32),
        in_specs=[pl.BlockSpec(memory_space=pltpu.VMEM)],
        out_specs=pl.BlockSpec(memory_space=pltpu.VMEM),
        scratch_shapes=scratch,
        compiler_params=pltpu.CompilerParams(
            collective_id=collective_id,
            has_side_effects=True,
            vmem_limit_bytes=16 * rows * cols + 4 * 1024 * 1024,
        ),
        cost_estimate=pl.CostEstimate(
            flops=rows * cols * 1_000, bytes_accessed=8 * rows * cols, transcendentals=0
        ),
        name="all_reduce_" + str(collective_id),
    )(x)


def cross_kernel(weight_ref, moments_ref, out_ref, high, rest):
    depth = moments_ref.shape[0]
    chunk = 128

    @pl.when(pl.program_id(0) == 0)
    def _():
        def body(i, carry):
            s = pl.ds(pl.multiple_of(i * chunk, chunk), chunk)
            value = moments_ref[s]
            top = value.astype(jnp.bfloat16)
            high[s] = top
            rest[s] = (value - top.astype(jnp.float32)).astype(jnp.bfloat16)
            return carry

        lax.fori_loop(0, depth // chunk, body, 0)

    rows = weight_ref[...]
    out_ref[...] = jnp.dot(rows, high[...], preferred_element_type=jnp.float32) + jnp.dot(
        rows, rest[...], preferred_element_type=jnp.float32
    )


def cross_product(weight, moments):
    rows, depth = weight.shape
    cols = moments.shape[1]
    tile = math.gcd(rows, 256)
    return pl.pallas_call(
        cross_kernel,
        grid=(rows // tile,),
        out_shape=jax.ShapeDtypeStruct((rows, cols), jnp.float32),
        in_specs=[
            pl.BlockSpec((tile, depth), lambda i: (i, 0)),
            pl.BlockSpec((depth, cols), lambda i: (0, 0)),
        ],
        out_specs=pl.BlockSpec((tile, cols), lambda i: (i, 0)),
        scratch_shapes=[pltpu.VMEM((depth, cols), jnp.bfloat16)] * 2,
        compiler_params=pltpu.CompilerParams(vmem_limit_bytes=24 * 1024 * 1024),
        cost_estimate=pl.CostEstimate(
            flops=4 * rows * depth * cols,
            bytes_accessed=2 * rows * depth + 4 * cols * (rows + depth),
            transcendentals=0,
        ),
        name="cross_product",
    )(weight, moments)


def shards(mesh, activations, weight, basis):
    tok, ch = mesh.shape["tok"], mesh.shape["ch"]
    partial_value = lax.dot_general(
        activations, basis, (((1,), (1,)), ((), ())), preferred_element_type=jnp.float32
    )
    codes = all_reduce(partial_value, "ch", ch, 2, 1)
    codes_low = codes.astype(jnp.bfloat16)
    half = codes.shape[1] // 2

    def moments_of(c):
        return lax.dot_general(
            activations,
            codes_low[:, c * half : (c + 1) * half],
            (((0,), (0,)), ((), ())),
            preferred_element_type=jnp.float32,
        )

    def cross_of(moments):
        return cross_product(weight, moments)

    def scatter(part):
        return lax.psum_scatter(part, "ch", scatter_dimension=0, tiled=True)

    first = cross_of(all_reduce(moments_of(0), "tok", tok, 4, 2))
    first, local = lax.optimization_barrier((first, moments_of(1)))
    cross_first = scatter(first)
    second = cross_of(all_reduce(local, "tok", tok, 4, 2))
    rank = codes.shape[1]
    local_gram = jnp.concatenate(
        [
            dot_f32(codes[:, j:], codes[:, j : j + pack], (((0,), (0,)), ((), ())))
            for j in range(0, rank, pack)
        ],
        axis=0,
    )
    second, local_gram = lax.optimization_barrier((second, local_gram))
    cross_second = scatter(second)
    gram = all_reduce(local_gram, "tok", tok, 4, 3)
    gram, cross_first = lax.optimization_barrier((gram, cross_first))
    inverse = inverse_factor(gram, rank)

    def high_dot(a, b, dims):
        return lax.dot_general(
            a, b, dims, precision=lax.Precision.HIGH, preferred_element_type=jnp.float32
        )

    middle = high_dot(cross_first, inverse[:, :half], NT) + high_dot(
        cross_second, inverse[:, half:], NT
    )
    return high_dot(middle, inverse, (((1,), (0,)), ((), ())))


def solution(mesh):
    in_specs = (P("tok", "ch"), P("tok", "ch"), P(None, "ch"))
    out_specs = P(("tok", "ch"), None)
    return jax.shard_map(
        functools.partial(shards, mesh),
        mesh=mesh,
        in_specs=in_specs,
        out_specs=out_specs,
        check_vma=False,
    )
```

```python
import functools
import math

import jax
import jax.numpy as jnp
from jax import lax
from jax.experimental import pallas as pl
from jax.experimental.pallas import tpu as pltpu
from jax.sharding import PartitionSpec as P

damping = 0.1
block = 128
group = 8
pack = 256
HIGHEST = lax.Precision.HIGHEST


def dot_f32(a, b, dims=(((1,), (0,)), ((), ()))):
    return lax.dot_general(a, b, dims, precision=HIGHEST, preferred_element_type=jnp.float32)


NT = (((1,), (1,)), ((), ()))


def factor_inverse(a):
    n = a.shape[0]
    tiles = n // 8
    lanes = lax.broadcasted_iota(jnp.int32, (8, n), 1)
    subs = lax.broadcasted_iota(jnp.int32, (8, n), 0)
    left = [a[8 * t : 8 * t + 8] for t in range(tiles)]
    right = [(lanes == subs + 8 * t).astype(jnp.float32) for t in range(tiles)]
    for start in range(0, n, group):
        first = start // 8
        base = start - 8 * first
        rows = [
            (left[first][base + g : base + g + 1], right[first][base + g : base + g + 1])
            for g in range(group)
        ]
        cols = {
            t: [
                jnp.broadcast_to(left[t][:, start + g : start + g + 1], (8, n))
                for g in range(group)
            ]
            for t in range(first, tiles)
        }
        small = [
            [cols[first][h][base + g : base + g + 1] for h in range(group)] for g in range(group)
        ]
        inverse = []
        factors = [[None] * group for _ in range(group)]
        for g in range(group):
            inverse.append(1.0 / small[g][g])
            for h in range(g + 1, group):
                f = small[h][g] * inverse[g]
                factors[h][g] = f
                for k in range(g + 1, group):
                    small[h][k] = small[h][k] - f * small[g][k]
                rows[h] = (rows[h][0] - f * rows[g][0], rows[h][1] - f * rows[g][1])
        scaled = [small[g] for g in range(group)]
        for t in range(first, tiles):
            mults = []
            for g in range(group):
                c = cols[t][g]
                for k in range(g):
                    c = c - mults[k] * scaled[k][g]
                m = c * inverse[g]
                if t == first:
                    m = jnp.where(subs > base + g, m, 0.0)
                mults.append(m)
            for g in range(group):
                left[t] = left[t] - mults[g] * rows[g][0]
                right[t] = right[t] - mults[g] * rows[g][1]
    out = []
    for t in range(tiles):
        pivot = jnp.sum(
            jnp.where(lanes == subs + 8 * t, left[t], 0.0), axis=1, keepdims=True
        )
        out.append(right[t] * (1.0 / jnp.sqrt(pivot)))
    return jnp.concatenate(out, axis=0)


def inverse_factor_kernel(packed_ref, out_ref, work, diag):
    n = work.shape[0]
    steps = n // block
    offset = 0
    for j in range(0, n, pack):
        work[j:, j : j + pack] = packed_ref[offset : offset + n - j]
        for i in range(j + pack, n, pack):
            at = offset + i - j
            work[j : j + pack, i : i + pack] = packed_ref[at : at + pack].T
        offset += n - j
    trace = jnp.zeros((1, 1), jnp.float32)
    eye = lax.broadcasted_iota(jnp.int32, (block, block), 0) == lax.broadcasted_iota(
        jnp.int32, (block, block), 1
    )
    for k in range(steps):
        s = slice(k * block, (k + 1) * block)
        trace += jnp.sum(jnp.where(eye, work[s, s], 0.0), keepdims=True)
    ridge = damping * trace / n
    for k in range(steps):
        s = slice(k * block, (k + 1) * block)
        work[s, s] = work[s, s] + jnp.where(eye, ridge, 0.0)

    def step(k, carry):
        o = pl.multiple_of(k * block, block)
        diag[...] = factor_inverse(work[pl.ds(o, block), pl.ds(o, block)])
        for kk in range(steps):

            @pl.when(k == kk)
            def _(kk=kk):
                s = slice(kk * block, (kk + 1) * block)
                inv = diag[...]
                row = dot_f32(inv, work[s, :])
                work[s, :] = row
                work[s, s] = inv
                row = work[s, :]
                if kk + 1 < steps:
                    below = slice((kk + 1) * block, n)
                    mult = dot_f32(work[below, s], inv, NT)
                    work[below, s] = jnp.zeros((n - (kk + 1) * block, block), jnp.float32)
                    work[below, :] = work[below, :] - dot_f32(mult, row)

        return carry

    lax.fori_loop(0, steps, step, 0)
    for k in range(steps):
        s = slice(k * block, (k + 1) * block)
        if k:
            out_ref[s, : k * block] = work[s, : k * block]
        out_ref[s, s] = work[s, s]
        if k + 1 < steps:
            out_ref[s, (k + 1) * block :] = jnp.zeros((block, n - (k + 1) * block), jnp.float32)


def inverse_factor(packed, n):
    return pl.pallas_call(
        inverse_factor_kernel,
        out_shape=jax.ShapeDtypeStruct((n, n), jnp.float32),
        in_specs=[pl.BlockSpec(memory_space=pltpu.VMEM)],
        out_specs=pl.BlockSpec(memory_space=pltpu.VMEM),
        scratch_shapes=[
            pltpu.VMEM((n, n), jnp.float32),
            pltpu.VMEM((block, block), jnp.float32),
        ],
        compiler_params=pltpu.CompilerParams(vmem_limit_bytes=32 * 1024 * 1024),
        cost_estimate=pl.CostEstimate(
            flops=1_000_000_000, bytes_accessed=8 * n * n, transcendentals=0
        ),
        name="inverse_factor",
    )(packed)


def all_reduce_kernel(axis, size, parts, x_ref, out_ref, acc, *rest):
    bits = size.bit_length() - 1
    land, (send, recv) = rest[:bits], rest[bits:]
    rows = x_ref.shape[0] // parts
    me = lax.axis_index(axis)
    bit = [lax.rem(me // (1 << b), 2) for b in range(bits)]
    peer = [me + (1 - 2 * bit[b]) * (1 << b) for b in range(bits)]

    barrier = pltpu.get_barrier_semaphore()
    for b in range(bits):
        pl.semaphore_signal(
            barrier, inc=1, device_id={axis: peer[b]}, device_id_type=pl.DeviceIdType.MESH
        )
    pl.semaphore_wait(barrier, bits)

    orders = []
    for p in range(parts):
        order = list(range(bits))
        if p % 2:
            order[-2:] = order[-2:][::-1]
        orders.append(order)
    starts = [[p * rows + jnp.int32(0)] for p in range(parts)]
    for p in range(parts):
        for s in range(bits):
            starts[p].append(starts[p][-1] + bit[orders[p][s]] * (rows >> (s + 1)))

    def copy(src, dst, p, s, phase):
        return pltpu.make_async_remote_copy(
            src_ref=src,
            dst_ref=dst,
            send_sem=send.at[phase, p, s],
            recv_sem=recv.at[phase, p, s],
            device_id={axis: peer[orders[p][s]]},
            device_id_type=pl.DeviceIdType.MESH,
        )

    def region(start, length):
        return pl.ds(pl.multiple_of(start, 8), length)

    def halve(p, s):
        length = rows >> (s + 1)
        away = starts[p][s] + (1 - bit[orders[p][s]]) * length
        src = x_ref if s == 0 else acc
        c = copy(src.at[region(away, length)], land[s].at[pl.ds(p * length, length)], p, s, 0)
        c.start()
        return c

    def add(p, s):
        length = rows >> (s + 1)
        src = x_ref if s == 0 else acc
        dst = out_ref if s == bits - 1 else acc
        chunk = math.gcd(length, 32)

        def body(i, carry):
            own = region(starts[p][s + 1] + i * chunk, chunk)
            dst[own] = src[own] + land[s][region(p * length + i * chunk, chunk)]
            return carry

        lax.fori_loop(0, length // chunk, body, 0)

    def double(p, s):
        own = region(starts[p][s + 1], rows >> (s + 1))
        c = copy(out_ref.at[own], out_ref.at[own], p, s, 1)
        c.start()
        return c

    started = []
    flying = [halve(p, 0) for p in range(parts)]
    for s in range(bits):
        for p in range(parts):
            flying[p].wait_recv()
            add(p, s)
            started.append(flying[p])
            flying[p] = halve(p, s + 1) if s + 1 < bits else double(p, s)
    for s in range(bits - 1, -1, -1):
        for p in range(parts):
            flying[p].wait_recv()
            started.append(flying[p])
            if s:
                flying[p] = double(p, s - 1)
    for c in started:
        c.wait_send()


def all_reduce(x, axis, size, most, collective_id):
    bits = size.bit_length() - 1
    rows, cols = x.shape
    parts = next(p for p in (most, most // 2) if rows % (8 * p * size) == 0)
    scratch = [pltpu.VMEM((rows, cols), jnp.float32)]
    scratch += [pltpu.VMEM((rows >> (s + 1), cols), jnp.float32) for s in range(bits)]
    scratch += [pltpu.SemaphoreType.DMA((2, parts, bits))] * 2
    return pl.pallas_call(
        functools.partial(all_reduce_kernel, axis, size, parts),
        out_shape=jax.ShapeDtypeStruct((rows, cols), jnp.float32),
        in_specs=[pl.BlockSpec(memory_space=pltpu.VMEM)],
        out_specs=pl.BlockSpec(memory_space=pltpu.VMEM),
        scratch_shapes=scratch,
        compiler_params=pltpu.CompilerParams(
            collective_id=collective_id,
            has_side_effects=True,
            vmem_limit_bytes=16 * rows * cols + 4 * 1024 * 1024,
        ),
        cost_estimate=pl.CostEstimate(
            flops=rows * cols * 1_000, bytes_accessed=8 * rows * cols, transcendentals=0
        ),
        name="all_reduce_" + str(collective_id),
    )(x)


def cross_kernel(weight_ref, moments_ref, out_ref, high, rest):
    depth = moments_ref.shape[0]
    chunk = 128

    @pl.when(pl.program_id(0) == 0)
    def _():
        def body(i, carry):
            s = pl.ds(pl.multiple_of(i * chunk, chunk), chunk)
            value = moments_ref[s]
            top = value.astype(jnp.bfloat16)
            high[s] = top
            rest[s] = (value - top.astype(jnp.float32)).astype(jnp.bfloat16)
            return carry

        lax.fori_loop(0, depth // chunk, body, 0)

    rows = weight_ref[...]
    out_ref[...] = jnp.dot(rows, high[...], preferred_element_type=jnp.float32) + jnp.dot(
        rows, rest[...], preferred_element_type=jnp.float32
    )


def cross_product(weight, moments):
    rows, depth = weight.shape
    cols = moments.shape[1]
    tile = math.gcd(rows, 256)
    return pl.pallas_call(
        cross_kernel,
        grid=(rows // tile,),
        out_shape=jax.ShapeDtypeStruct((rows, cols), jnp.float32),
        in_specs=[
            pl.BlockSpec((tile, depth), lambda i: (i, 0)),
            pl.BlockSpec((depth, cols), lambda i: (0, 0)),
        ],
        out_specs=pl.BlockSpec((tile, cols), lambda i: (i, 0)),
        scratch_shapes=[pltpu.VMEM((depth, cols), jnp.bfloat16)] * 2,
        compiler_params=pltpu.CompilerParams(vmem_limit_bytes=24 * 1024 * 1024),
        cost_estimate=pl.CostEstimate(
            flops=4 * rows * depth * cols,
            bytes_accessed=2 * rows * depth + 4 * cols * (rows + depth),
            transcendentals=0,
        ),
        name="cross_product",
    )(weight, moments)


def shards(mesh, activations, weight, basis):
    tok, ch = mesh.shape["tok"], mesh.shape["ch"]
    partial_value = lax.dot_general(
        activations, basis, (((1,), (1,)), ((), ())), preferred_element_type=jnp.float32
    )
    codes = all_reduce(partial_value, "ch", ch, 4, 1)
    codes_low = codes.astype(jnp.bfloat16)
    half = codes.shape[1] // 2

    def moments_of(c):
        return lax.dot_general(
            activations,
            codes_low[:, c * half : (c + 1) * half],
            (((0,), (0,)), ((), ())),
            preferred_element_type=jnp.float32,
        )

    def cross_of(moments):
        return cross_product(weight, moments)

    def scatter(part):
        return lax.psum_scatter(part, "ch", scatter_dimension=0, tiled=True)

    first = cross_of(all_reduce(moments_of(0), "tok", tok, 8, 2))
    first, local = lax.optimization_barrier((first, moments_of(1)))
    cross_first = scatter(first)
    second = cross_of(all_reduce(local, "tok", tok, 8, 2))
    rank = codes.shape[1]
    local_gram = jnp.concatenate(
        [
            dot_f32(codes[:, j:], codes[:, j : j + pack], (((0,), (0,)), ((), ())))
            for j in range(0, rank, pack)
        ],
        axis=0,
    )
    second, local_gram = lax.optimization_barrier((second, local_gram))
    cross_second = scatter(second)
    gram = all_reduce(local_gram, "tok", tok, 8, 3)
    gram, cross_first = lax.optimization_barrier((gram, cross_first))
    inverse = inverse_factor(gram, rank)

    def high_dot(a, b, dims):
        return lax.dot_general(
            a, b, dims, precision=lax.Precision.HIGH, preferred_element_type=jnp.float32
        )

    middle = high_dot(cross_first, inverse[:, :half], NT) + high_dot(
        cross_second, inverse[:, half:], NT
    )
    return high_dot(middle, inverse, (((1,), (0,)), ((), ())))


def solution(mesh):
    in_specs = (P("tok", "ch"), P("tok", "ch"), P(None, "ch"))
    out_specs = P(("tok", "ch"), None)
    return jax.shard_map(
        functools.partial(shards, mesh),
        mesh=mesh,
        in_specs=in_specs,
        out_specs=out_specs,
        check_vma=False,
    )
```
